256 devices in a mesh: pipe: 64 (over y, x, z_hi, core), tp: 4 (over z_lo).
Axes of the slice: x: 4, y: 4, z: 8 (z_hi: 2, z_lo: 4; z = z_hi * 4 + z_lo), core: 2. Of those that a mesh axis runs over, the one named last changes fastest.
Arguments:
- checkpoint: bfloat16 [64, 3, 512, 6144], P('pipe', None, 'tp'), may hold values from -6 to 6
- grad_out: bfloat16 [64, 512, 6144], P('pipe', 'tp'), may hold values from -6 to 6
Outputs:
- qkv_grad: bfloat16 [64, 3, 512, 6144], P('pipe', None, 'tp')
The draws below stay inside these ranges and needn't reach their ends.
All inputs are finite; a program needn't handle non-finite values.
Results may differ from the reference program's by a relative error of at most 0.0087.
Values may be sent and summed in bfloat16 or wider, within the bound.
A program may use at most 128 MiB of HBM per device.

```python
import jax
import jax.numpy as jnp
from jax import lax

HEAD_DIM = 128
TOKENS = 512
WIDTH = 6144
N_PIPE = 64


def draw_checkpoint(key, part):
    key = jax.random.fold_in(key, 11)
    shape = (N_PIPE, 3, TOKENS, WIDTH)
    first = jax.random.fold_in(key, 0)
    base = jnp.clip(jax.random.normal(first, shape, jnp.float32), -6.0, 6.0)
    return base.astype(jnp.bfloat16)


def level_of(own_key, extent, shards, smallest, high):
    factor_of = 1.0
    for axis_at, parts in shards:
        heights = jax.random.uniform(jax.random.fold_in(jax.random.fold_in(own_key, 6), axis_at), (parts,), jnp.float32, smallest / len(shards), high / len(shards))
        factor_of = factor_of * jnp.repeat(jnp.exp(heights), extent[axis_at] // parts).reshape((-1,) + (1,) * (len(extent) - 1 - axis_at))
    return factor_of


def gaussian(rng, dims, spread, most, cuts=(), dtype=jnp.bfloat16):
    level = level_of(rng, dims, cuts, -0.22, 0.18) if cuts else 1.0
    entries = jax.random.normal(rng, dims, jnp.float32) * spread * level
    return jnp.minimum(jnp.maximum(entries, -most), most).astype(dtype)


def setup_inputs(seed: int = 0) -> dict:
    key_of = jax.random.split(jax.random.key(seed), 3)
    checkpoint = draw_checkpoint(jax.random.fold_in(key_of[2], 71), 0)
    grad_out = gaussian(key_of[1], (N_PIPE, TOKENS, WIDTH), 1.0, 6.0, ((0, 64), (1, 4)))
    return {"checkpoint": checkpoint, "grad_out": grad_out}


def attend_back(block, grad_rows, head_dim):
    length = block.shape[1]
    heads = block.shape[2] // head_dim
    scale = head_dim ** -0.5
    query = block[0].reshape(length, heads, head_dim).astype(jnp.float32)
    keys = block[1].reshape(length, heads, head_dim).astype(jnp.float32)
    values = block[2].reshape(length, heads, head_dim).astype(jnp.float32)
    grads = grad_rows.reshape(length, heads, head_dim).astype(jnp.float32)
    scores = jnp.einsum("qhd,khd->hqk", query, keys) * scale
    rows = lax.broadcasted_iota(jnp.int32, (length, length), 0)
    cols = lax.broadcasted_iota(jnp.int32, (length, length), 1)
    scores = jnp.where((cols <= rows)[None], scores, jnp.float32(-1e30))
    top = jnp.max(scores, axis=-1, keepdims=True)
    expd = jnp.exp(scores - top)
    probs = expd / jnp.sum(expd, axis=-1, keepdims=True)
    probs_b = lax.optimization_barrier(probs.astype(jnp.bfloat16)).astype(jnp.float32)
    attn = jnp.einsum("hqk,khd->qhd", probs_b, values)
    dprobs = jnp.einsum("qhd,khd->hqk", grads, values)
    delta = jnp.transpose(jnp.sum(grads * attn, axis=-1))[:, :, None]
    dscores = lax.optimization_barrier((probs * (dprobs - delta) * scale).astype(jnp.bfloat16)).astype(jnp.float32)
    dquery = jnp.einsum("hqk,khd->qhd", dscores, keys)
    dkeys = jnp.einsum("hqk,qhd->khd", dscores, query)
    dvalues = jnp.einsum("hqk,qhd->khd", probs_b, grads)
    stacked = jnp.stack([dquery, dkeys, dvalues], axis=0).reshape(3, length, heads * head_dim)
    return stacked.astype(jnp.bfloat16)


def one_section(inputs):
    block, grad_rows = inputs
    return attend_back(block, grad_rows, HEAD_DIM)


def reference(checkpoint, grad_out):
    block = jnp.flip(checkpoint, axis=0)
    return lax.map(one_section, (block, grad_out))
```

```python
import functools

import jax
import jax.numpy as jnp
from jax import lax
from jax.experimental import pallas as pl
from jax.experimental.pallas import tpu as pltpu
from jax.sharding import PartitionSpec as P

HEAD_DIM = 128
MESH = pl.DeviceIdType.MESH
AHEAD = 3
NT = (((1,), (1,)), ((), ()))
NN = (((1,), (0,)), ((), ()))
TN = (((0,), (0,)), ((), ()))


def dot(a, b, dims):
    return lax.dot_general(a, b, dims, preferred_element_type=jnp.float32)


def head_back(q, k, v, g):
    length = q.shape[0]
    scale = HEAD_DIM ** (-0.5)
    scores = dot(q, k, NT) * scale
    rows = lax.broadcasted_iota(jnp.int32, (length, length), 0)
    cols = lax.broadcasted_iota(jnp.int32, (length, length), 1)
    scores = jnp.where(cols <= rows, scores, jnp.float32(-1e30))
    top = jnp.max(scores, axis=-1, keepdims=True)
    expd = jnp.exp(scores - top)
    probs = expd / jnp.sum(expd, axis=-1, keepdims=True)
    probs_b = probs.astype(jnp.bfloat16)
    dprobs = dot(g, v, NT)
    delta = jnp.sum(probs_b.astype(jnp.float32) * dprobs, axis=-1, keepdims=True)
    dscores = (probs * (dprobs - delta) * scale).astype(jnp.bfloat16)
    dq = dot(dscores, k, NN)
    dk = dot(dscores, q, TN)
    dv = dot(probs_b, g, TN)
    return dq, dk, dv


def kernel(sections, ranks, ckpt, grad, out, qkv, gbuf, obuf, msend, mrecv, gsend, grecv, osend, orecv):
    p = lax.axis_index("pipe")
    t = lax.axis_index("tp")
    mirror = sections - 1 - p
    rows = ckpt.shape[1]
    owned = ckpt.shape[2] // ranks
    chunks = qkv.shape[0]
    width = qkv.shape[3]
    mine = pl.ds(pl.multiple_of(t * rows, rows), rows)

    def peer(k):
        return lax.rem(t + k, ranks)

    def features(rank, c):
        return pl.ds(pl.multiple_of(rank * owned + c * width, width), width)

    barrier = pltpu.get_barrier_semaphore()
    for k in range(ranks):
        pl.semaphore_signal(barrier, inc=1, device_id=(mirror, peer(k)), device_id_type=MESH)
    for k in range(1, ranks):
        pl.semaphore_signal(barrier, inc=1, device_id=(p, peer(k)), device_id_type=MESH)
    pl.semaphore_wait(barrier, 2 * ranks - 1)

    def fetch(c):
        pltpu.make_async_copy(grad.at[:, features(t, c)], gbuf.at[c, mine, :], grecv.at[c]).start()
        for k in range(ranks):
            pltpu.make_async_remote_copy(
                src_ref=ckpt.at[:, :, features(peer(k), c)],
                dst_ref=qkv.at[c, :, mine, :],
                send_sem=msend,
                recv_sem=mrecv.at[c],
                device_id=(mirror, peer(k)),
                device_id_type=MESH,
            ).start()
        for k in range(1, ranks):
            pltpu.make_async_remote_copy(
                src_ref=grad.at[:, features(peer(k), c)],
                dst_ref=gbuf.at[c, mine, :],
                send_sem=gsend,
                recv_sem=grecv.at[c],
                device_id=(p, peer(k)),
                device_id_type=MESH,
            ).start()

    def arrived(ref, sem):
        pltpu.make_async_copy(ref, ref, sem).wait()

    for c in range(AHEAD):
        fetch(c)

    @pl.loop(0, chunks)
    def _(c):
        arrived(qkv.at[c], mrecv.at[c])
        arrived(gbuf.at[c], grecv.at[c])

        @pl.when(c + AHEAD < chunks)
        def _():
            fetch(c + AHEAD)

        for h in range(width // HEAD_DIM):
            lanes = slice(h * HEAD_DIM, (h + 1) * HEAD_DIM)
            dq, dk, dv = head_back(qkv[c, 0, :, lanes], qkv[c, 1, :, lanes], qkv[c, 2, :, lanes], gbuf[c, :, lanes])
            obuf[c, 0, :, lanes] = dq.astype(jnp.bfloat16)
            obuf[c, 1, :, lanes] = dk.astype(jnp.bfloat16)
            obuf[c, 2, :, lanes] = dv.astype(jnp.bfloat16)

        for k in range(1, ranks):
            theirs = pl.ds(pl.multiple_of(peer(k) * rows, rows), rows)
            pltpu.make_async_remote_copy(
                src_ref=obuf.at[c, :, theirs, :],
                dst_ref=out.at[:, :, features(t, c)],
                send_sem=osend,
                recv_sem=orecv,
                device_id=(p, peer(k)),
                device_id_type=MESH,
            ).start()
        pltpu.make_async_copy(obuf.at[c, :, mine, :], out.at[:, :, features(t, c)], orecv).start()

    arrived(ckpt, msend)
    most = pl.ds(0, (ranks - 1) * owned)
    arrived(grad.at[:, most], gsend)
    arrived(out.at[:, :, most], osend)
    arrived(out, orecv)


def on_device(ckpt, grad, width=HEAD_DIM):
    sections = lax.axis_size("pipe")
    ranks = lax.axis_size("tp")
    _, parts, rows, features = ckpt.shape
    length = rows * ranks
    owned = features // ranks
    chunks = owned // width
    out = pl.pallas_call(
        functools.partial(kernel, sections, ranks),
        out_shape=jax.ShapeDtypeStruct((parts, rows, features), jnp.bfloat16),
        in_specs=[pl.BlockSpec(memory_space=pl.ANY)] * 2,
        out_specs=pl.BlockSpec(memory_space=pl.ANY),
        scratch_shapes=[
            pltpu.VMEM((chunks, parts, length, width), jnp.bfloat16),
            pltpu.VMEM((chunks, length, width), jnp.bfloat16),
            pltpu.VMEM((chunks, parts, length, width), jnp.bfloat16),
            pltpu.SemaphoreType.DMA,
            pltpu.SemaphoreType.DMA((chunks,)),
            pltpu.SemaphoreType.DMA,
            pltpu.SemaphoreType.DMA((chunks,)),
            pltpu.SemaphoreType.DMA,
            pltpu.SemaphoreType.DMA,
        ],
        compiler_params=pltpu.CompilerParams(
            collective_id=0, has_side_effects=True, vmem_limit_bytes=56 * 2**20
        ),
    )(ckpt[0], grad[0])
    return out[None]


def solution(mesh):
    in_specs = (P("pipe", None, "tp", None), P("pipe", "tp", None))
    out_specs = P("pipe", None, "tp", None)
    return jax.shard_map(
        on_device, mesh=mesh, in_specs=in_specs, out_specs=out_specs, check_vma=False
    )
```

```python
import functools

import jax
import jax.numpy as jnp
from jax import lax
from jax.experimental import pallas as pl
from jax.experimental.pallas import tpu as pltpu
from jax.sharding import PartitionSpec as P

HEAD_DIM = 128
MESH = pl.DeviceIdType.MESH
EARLY = 3
LIMIT = 59
NT = (((1,), (1,)), ((), ()))
NN = (((1,), (0,)), ((), ()))
TN = (((0,), (0,)), ((), ()))


def dot(a, b, dims):
    return lax.dot_general(a, b, dims, preferred_element_type=jnp.float32)


def head_back(q, k, v, g):
    length = q.shape[0]
    scale = HEAD_DIM ** (-0.5)
    scores = dot(q, k, NT) * scale
    rows = lax.broadcasted_iota(jnp.int32, (length, length), 0)
    cols = lax.broadcasted_iota(jnp.int32, (length, length), 1)
    scores = jnp.where(cols <= rows, scores, jnp.float32(-1e30))
    top = jnp.max(scores, axis=-1, keepdims=True)
    expd = jnp.exp(scores - top)
    probs = expd / jnp.sum(expd, axis=-1, keepdims=True)
    probs_b = probs.astype(jnp.bfloat16)
    dprobs = dot(g, v, NT)
    delta = jnp.sum(probs_b.astype(jnp.float32) * dprobs, axis=-1, keepdims=True)
    dscores = (probs * (dprobs - delta) * scale).astype(jnp.bfloat16)
    dq = dot(dscores, k, NN)
    dk = dot(dscores, q, TN)
    dv = dot(probs_b, g, TN)
    return dq, dk, dv


def kernel(sections, ranks, ckpt, grad, out, qkv, gbuf, obuf, msend, mrecv, gsend, grecv, osend, orecv, ready):
    p = lax.axis_index("pipe")
    t = lax.axis_index("tp")
    mirror = sections - 1 - p
    rows = ckpt.shape[1]
    owned = ckpt.shape[2] // ranks
    chunks = qkv.shape[0]
    width = qkv.shape[3]
    mine = pl.ds(pl.multiple_of(t * rows, rows), rows)

    def peer(k):
        return lax.rem(t + k, ranks)

    def features(rank, c):
        return pl.ds(pl.multiple_of(rank * owned + c * width, width), width)

    def fetch_grad(c):
        pltpu.make_async_copy(grad.at[:, features(t, c)], gbuf.at[c, mine, :], grecv.at[c]).start()
        for k in range(1, ranks):
            pltpu.make_async_remote_copy(
                src_ref=grad.at[:, features(peer(k), c)],
                dst_ref=gbuf.at[c, mine, :],
                send_sem=gsend,
                recv_sem=grecv.at[c],
                device_id=(p, peer(k)),
                device_id_type=MESH,
            ).start()

    def fetch_mirror(c):
        for k in range(ranks):
            pltpu.make_async_remote_copy(
                src_ref=ckpt.at[:, :, features(peer(k), c)],
                dst_ref=qkv.at[c, :, mine, :],
                send_sem=msend,
                recv_sem=mrecv.at[c],
                device_id=(mirror, peer(k)),
                device_id_type=MESH,
            ).start()

    upper = lax.rem(lax.div(p, 2), 2)
    barrier = pltpu.get_barrier_semaphore()
    for k in range(1, ranks):
        pl.semaphore_signal(barrier, inc=1, device_id=(p, peer(k)), device_id_type=MESH)

    @pl.when(upper == 0)
    def _():
        for k in range(ranks):
            pl.semaphore_signal(barrier, inc=1, device_id=(mirror, peer(k)), device_id_type=MESH)
        pl.semaphore_wait(barrier, ranks - 1)

    @pl.when(upper == 1)
    def _():
        pl.semaphore_wait(barrier, 2 * ranks - 1)
        for k in range(ranks):
            pl.semaphore_signal(ready, inc=1, device_id=(mirror, peer(k)), device_id_type=MESH)

    for c in range(EARLY):
        fetch_grad(c)

    @pl.when(upper == 0)
    def _():
        pl.semaphore_wait(ready, ranks)

    @pl.loop(0, chunks)
    def _(c):
        fetch_mirror(c)

        @pl.when(c + EARLY < chunks)
        def _():
            fetch_grad(c + EARLY)

    def arrived(ref, sem):
        pltpu.make_async_copy(ref, ref, sem).wait()

    @pl.loop(0, chunks)
    def _(c):
        arrived(qkv.at[c], mrecv.at[c])
        arrived(gbuf.at[c], grecv.at[c])

        for h in range(width // HEAD_DIM):
            lanes = slice(h * HEAD_DIM, (h + 1) * HEAD_DIM)
            dq, dk, dv = head_back(qkv[c, 0, :, lanes], qkv[c, 1, :, lanes], qkv[c, 2, :, lanes], gbuf[c, :, lanes])
            obuf[c, 0, :, lanes] = dq.astype(jnp.bfloat16)
            obuf[c, 1, :, lanes] = dk.astype(jnp.bfloat16)
            obuf[c, 2, :, lanes] = dv.astype(jnp.bfloat16)

        for k in range(1, ranks):
            theirs = pl.ds(pl.multiple_of(peer(k) * rows, rows), rows)
            pltpu.make_async_remote_copy(
                src_ref=obuf.at[c, :, theirs, :],
                dst_ref=out.at[:, :, features(t, c)],
                send_sem=osend,
                recv_sem=orecv,
                device_id=(p, peer(k)),
                device_id_type=MESH,
            ).start()
        pltpu.make_async_copy(obuf.at[c, :, mine, :], out.at[:, :, features(t, c)], orecv).start()

    arrived(ckpt, msend)
    most = pl.ds(0, (ranks - 1) * owned)
    arrived(grad.at[:, most], gsend)
    arrived(out.at[:, :, most], osend)
    arrived(out, orecv)


def on_device(ckpt, grad, width=HEAD_DIM):
    sections = lax.axis_size("pipe")
    ranks = lax.axis_size("tp")
    _, parts, rows, features = ckpt.shape
    length = rows * ranks
    owned = features // ranks
    chunks = owned // width
    out = pl.pallas_call(
        functools.partial(kernel, sections, ranks),
        out_shape=pltpu.VMEM((parts, rows, features), jnp.bfloat16),
        in_specs=[pl.BlockSpec(memory_space=pl.ANY)] * 2,
        out_specs=pl.BlockSpec(memory_space=pltpu.VMEM),
        scratch_shapes=[
            pltpu.VMEM((chunks, parts, length, width), jnp.bfloat16),
            pltpu.VMEM((chunks, length, width), jnp.bfloat16),
            pltpu.VMEM((chunks, parts, length, width), jnp.bfloat16),
            pltpu.SemaphoreType.DMA,
            pltpu.SemaphoreType.DMA((chunks,)),
            pltpu.SemaphoreType.DMA,
            pltpu.SemaphoreType.DMA((chunks,)),
            pltpu.SemaphoreType.DMA,
            pltpu.SemaphoreType.DMA,
            pltpu.SemaphoreType.REGULAR,
        ],
        compiler_params=pltpu.CompilerParams(
            collective_id=0, has_side_effects=True, vmem_limit_bytes=LIMIT * 2**20
        ),
    )(ckpt[0], grad[0])
    return out[None]


def solution(mesh):
    in_specs = (P("pipe", None, "tp", None), P("pipe", "tp", None))
    out_specs = P("pipe", None, "tp", None)
    return jax.shard_map(
        on_device, mesh=mesh, in_specs=in_specs, out_specs=out_specs, check_vma=False
    )
```

```python
import functools

import jax
import jax.numpy as jnp
from jax import lax
from jax.experimental import pallas as pl
from jax.experimental.pallas import tpu as pltpu
from jax.sharding import PartitionSpec as P

HEAD_DIM = 128
MESH = pl.DeviceIdType.MESH
EARLY = 3
PACE = 3
NT = (((1,), (1,)), ((), ()))
NN = (((1,), (0,)), ((), ()))
TN = (((0,), (0,)), ((), ()))


def dot(a, b, dims):
    return lax.dot_general(a, b, dims, preferred_element_type=jnp.float32)


def head_back(q, k, v, g):
    length = q.shape[0]
    scale = HEAD_DIM ** (-0.5)
    scores = dot(q, k, NT) * scale
    rows = lax.broadcasted_iota(jnp.int32, (length, length), 0)
    cols = lax.broadcasted_iota(jnp.int32, (length, length), 1)
    scores = jnp.where(cols <= rows, scores, jnp.float32(-1e30))
    top = jnp.max(scores, axis=-1, keepdims=True)
    expd = jnp.exp(scores - top)
    probs = expd / jnp.sum(expd, axis=-1, keepdims=True)
    probs_b = probs.astype(jnp.bfloat16)
    dprobs = dot(g, v, NT)
    delta = jnp.sum(probs_b.astype(jnp.float32) * dprobs, axis=-1, keepdims=True)
    dscores = (probs * (dprobs - delta) * scale).astype(jnp.bfloat16)
    dq = dot(dscores, k, NN)
    dk = dot(dscores, q, TN)
    dv = dot(probs_b, g, TN)
    return dq, dk, dv


def kernel(sections, ranks, ckpt, grad, out, qkv, gbuf, obuf, msend, mrecv, gsend, grecv, osend, orecv, ready):
    p = lax.axis_index("pipe")
    t = lax.axis_index("tp")
    mirror = sections - 1 - p
    rows = ckpt.shape[1]
    owned = ckpt.shape[2] // ranks
    chunks = qkv.shape[0]
    width = qkv.shape[3]
    mine = pl.ds(pl.multiple_of(t * rows, rows), rows)

    def peer(k):
        return lax.rem(t + k, ranks)

    def features(rank, c):
        return pl.ds(pl.multiple_of(rank * owned + c * width, width), width)

    def fetch_grad(c):
        pltpu.make_async_copy(grad.at[:, features(t, c)], gbuf.at[c, mine, :], grecv.at[c]).start()
        for k in range(1, ranks):
            pltpu.make_async_remote_copy(
                src_ref=grad.at[:, features(peer(k), c)],
                dst_ref=gbuf.at[c, mine, :],
                send_sem=gsend,
                recv_sem=grecv.at[c],
                device_id=(p, peer(k)),
                device_id_type=MESH,
            ).start()

    def fetch_mirror(c):
        for k in range(ranks):
            pltpu.make_async_remote_copy(
                src_ref=ckpt.at[:, :, features(peer(k), c)],
                dst_ref=qkv.at[c, :, mine, :],
                send_sem=msend,
                recv_sem=mrecv.at[c],
                device_id=(mirror, peer(k)),
                device_id_type=MESH,
            ).start()

    place = lax.div(p, 16) + lax.rem(lax.div(p, 4), 4)
    half = lax.rem(lax.div(p, 2), 2)
    answers = 2 * place + 7 * half >= 10
    barrier = pltpu.get_barrier_semaphore()
    for k in range(1, ranks):
        pl.semaphore_signal(barrier, inc=1, device_id=(p, peer(k)), device_id_type=MESH)

    @pl.when(jnp.logical_not(answers))
    def _():
        for k in range(ranks):
            pl.semaphore_signal(barrier, inc=1, device_id=(mirror, peer(k)), device_id_type=MESH)
        pl.semaphore_wait(barrier, ranks - 1)

    @pl.when(answers)
    def _():
        pl.semaphore_wait(barrier, 2 * ranks - 1)
        for k in range(ranks):
            pl.semaphore_signal(ready, inc=1, device_id=(mirror, peer(k)), device_id_type=MESH)

    for c in range(EARLY):
        fetch_grad(c)

    @pl.when(jnp.logical_not(answers))
    def _():
        pl.semaphore_wait(ready, ranks)

    @pl.loop(0, chunks)
    def _(c):
        fetch_mirror(c)

        for j in range(PACE):
            @pl.when(EARLY + c * PACE + j < chunks)
            def _():
                fetch_grad(EARLY + c * PACE + j)

    def arrived(ref, sem):
        pltpu.make_async_copy(ref, ref, sem).wait()

    @pl.loop(0, chunks)
    def _(c):
        arrived(qkv.at[c], mrecv.at[c])
        arrived(gbuf.at[c], grecv.at[c])

        for h in range(width // HEAD_DIM):
            lanes = slice(h * HEAD_DIM, (h + 1) * HEAD_DIM)
            dq, dk, dv = head_back(qkv[c, 0, :, lanes], qkv[c, 1, :, lanes], qkv[c, 2, :, lanes], gbuf[c, :, lanes])
            obuf[c, 0, :, lanes] = dq.astype(jnp.bfloat16)
            obuf[c, 1, :, lanes] = dk.astype(jnp.bfloat16)
            obuf[c, 2, :, lanes] = dv.astype(jnp.bfloat16)

        for k in range(1, ranks):
            theirs = pl.ds(pl.multiple_of(peer(k) * rows, rows), rows)
            pltpu.make_async_remote_copy(
                src_ref=obuf.at[c, :, theirs, :],
                dst_ref=out.at[:, :, features(t, c)],
                send_sem=osend,
                recv_sem=orecv,
                device_id=(p, peer(k)),
                device_id_type=MESH,
            ).start()
        pltpu.make_async_copy(obuf.at[c, :, mine, :], out.at[:, :, features(t, c)], orecv).start()

    arrived(ckpt, msend)
    most = pl.ds(0, (ranks - 1) * owned)
    arrived(grad.at[:, most], gsend)
    arrived(out.at[:, :, most], osend)
    arrived(out, orecv)


def on_device(ckpt, grad, width=HEAD_DIM):
    sections = lax.axis_size("pipe")
    ranks = lax.axis_size("tp")
    _, parts, rows, features = ckpt.shape
    length = rows * ranks
    owned = features // ranks
    chunks = owned // width
    out = pl.pallas_call(
        functools.partial(kernel, sections, ranks),
        out_shape=pltpu.VMEM((parts, rows, features), jnp.bfloat16),
        in_specs=[pl.BlockSpec(memory_space=pl.ANY)] * 2,
        out_specs=pl.BlockSpec(memory_space=pltpu.VMEM),
        scratch_shapes=[
            pltpu.VMEM((chunks, parts, length, width), jnp.bfloat16),
            pltpu.VMEM((chunks, length, width), jnp.bfloat16),
            pltpu.VMEM((chunks, parts, length, width), jnp.bfloat16),
            pltpu.SemaphoreType.DMA,
            pltpu.SemaphoreType.DMA((chunks,)),
            pltpu.SemaphoreType.DMA,
            pltpu.SemaphoreType.DMA((chunks,)),
            pltpu.SemaphoreType.DMA,
            pltpu.SemaphoreType.DMA,
            pltpu.SemaphoreType.REGULAR,
        ],
        compiler_params=pltpu.CompilerParams(
            collective_id=0, has_side_effects=True, vmem_limit_bytes=59 * 2**20
        ),
    )(ckpt[0], grad[0])
    return out[None]


def solution(mesh):
    in_specs = (P("pipe", None, "tp", None), P("pipe", "tp", None))
    out_specs = P("pipe", None, "tp", None)
    return jax.shard_map(
        on_device, mesh=mesh, in_specs=in_specs, out_specs=out_specs, check_vma=False
    )
```

```python
import functools

import jax
import jax.numpy as jnp
from jax import lax
from jax.experimental import pallas as pl
from jax.experimental.pallas import tpu as pltpu
from jax.sharding import PartitionSpec as P

HEAD_DIM = 128
MESH = pl.DeviceIdType.MESH
EARLY = 3
PACE = 3
NT = (((1,), (1,)), ((), ()))
NN = (((1,), (0,)), ((), ()))
TN = (((0,), (0,)), ((), ()))


def dot(a, b, dims):
    return lax.dot_general(a, b, dims, preferred_element_type=jnp.float32)


def head_back(q, k, v, g):
    length = q.shape[0]
    scale = HEAD_DIM ** (-0.5)
    scores = dot(q, k, NT) * scale
    rows = lax.broadcasted_iota(jnp.int32, (length, length), 0)
    cols = lax.broadcasted_iota(jnp.int32, (length, length), 1)
    scores = jnp.where(cols <= rows, scores, jnp.float32(-1e30))
    top = jnp.max(scores, axis=-1, keepdims=True)
    expd = jnp.exp(scores - top)
    probs = expd / jnp.sum(expd, axis=-1, keepdims=True)
    probs_b = probs.astype(jnp.bfloat16)
    dprobs = dot(g, v, NT)
    delta = jnp.sum(probs_b.astype(jnp.float32) * dprobs, axis=-1, keepdims=True)
    dscores = (probs * (dprobs - delta) * scale).astype(jnp.bfloat16)
    dq = dot(dscores, k, NN)
    dk = dot(dscores, q, TN)
    dv = dot(probs_b, g, TN)
    return dq, dk, dv


def kernel(sections, ranks, ckpt, grad, out, qkv, gbuf, obuf, msend, mrecv, gsend, grecv, osend, orecv, ready):
    p = lax.axis_index("pipe")
    t = lax.axis_index("tp")
    mirror = sections - 1 - p
    rows = ckpt.shape[1]
    owned = ckpt.shape[2] // ranks
    chunks = qkv.shape[0]
    width = qkv.shape[3]
    mine = pl.ds(pl.multiple_of(t * rows, rows), rows)

    def peer(k):
        return lax.rem(t + k, ranks)

    def features(rank, c):
        return pl.ds(pl.multiple_of(rank * owned + c * width, width), width)

    def fetch_grad(c):
        pltpu.make_async_copy(grad.at[:, features(t, c)], gbuf.at[c, mine, :], grecv.at[c]).start()
        for k in range(1, ranks):
            pltpu.make_async_remote_copy(
                src_ref=grad.at[:, features(peer(k), c)],
                dst_ref=gbuf.at[c, mine, :],
                send_sem=gsend,
                recv_sem=grecv.at[c],
                device_id=(p, peer(k)),
                device_id_type=MESH,
            ).start()

    def fetch_mirror(c):
        for k in range(ranks):
            pltpu.make_async_remote_copy(
                src_ref=ckpt.at[:, :, features(peer(k), c)],
                dst_ref=qkv.at[c, :, mine, :],
                send_sem=msend,
                recv_sem=mrecv.at[c],
                device_id=(mirror, peer(k)),
                device_id_type=MESH,
            ).start()

    place = lax.div(p, 16) + lax.rem(lax.div(p, 4), 4)
    half = lax.rem(lax.div(p, 2), 2)
    answers = 2 * place + 9 * half >= 11
    barrier = pltpu.get_barrier_semaphore()
    for k in range(1, ranks):
        pl.semaphore_signal(barrier, inc=1, device_id=(p, peer(k)), device_id_type=MESH)

    @pl.when(jnp.logical_not(answers))
    def _():
        for k in range(ranks):
            pl.semaphore_signal(barrier, inc=1, device_id=(mirror, peer(k)), device_id_type=MESH)
        pl.semaphore_wait(barrier, ranks - 1)

    @pl.when(answers)
    def _():
        pl.semaphore_wait(barrier, 2 * ranks - 1)
        for k in range(ranks):
            pl.semaphore_signal(ready, inc=1, device_id=(mirror, peer(k)), device_id_type=MESH)

    for c in range(EARLY):
        fetch_grad(c)

    @pl.when(jnp.logical_not(answers))
    def _():
        pl.semaphore_wait(ready, ranks)

    @pl.loop(0, chunks)
    def _(c):
        fetch_mirror(c)

        for j in range(PACE):
            @pl.when(EARLY + c * PACE + j < chunks)
            def _():
                fetch_grad(EARLY + c * PACE + j)

    def arrived(ref, sem):
        pltpu.make_async_copy(ref, ref, sem).wait()

    @pl.loop(0, chunks)
    def _(c):
        arrived(qkv.at[c], mrecv.at[c])
        arrived(gbuf.at[c], grecv.at[c])

        for h in range(width // HEAD_DIM):
            lanes = slice(h * HEAD_DIM, (h + 1) * HEAD_DIM)
            dq, dk, dv = head_back(qkv[c, 0, :, lanes], qkv[c, 1, :, lanes], qkv[c, 2, :, lanes], gbuf[c, :, lanes])
            obuf[c, 0, :, lanes] = dq.astype(jnp.bfloat16)
            obuf[c, 1, :, lanes] = dk.astype(jnp.bfloat16)
            obuf[c, 2, :, lanes] = dv.astype(jnp.bfloat16)

        for k in range(1, ranks):
            theirs = pl.ds(pl.multiple_of(peer(k) * rows, rows), rows)
            pltpu.make_async_remote_copy(
                src_ref=obuf.at[c, :, theirs, :],
                dst_ref=out.at[:, :, features(t, c)],
                send_sem=osend,
                recv_sem=orecv,
                device_id=(p, peer(k)),
                device_id_type=MESH,
            ).start()
        pltpu.make_async_copy(obuf.at[c, :, mine, :], out.at[:, :, features(t, c)], orecv).start()

    arrived(ckpt, msend)
    most = pl.ds(0, (ranks - 1) * owned)
    arrived(grad.at[:, most], gsend)
    arrived(out.at[:, :, most], osend)
    arrived(out, orecv)


def on_device(ckpt, grad, width=HEAD_DIM):
    sections = lax.axis_size("pipe")
    ranks = lax.axis_size("tp")
    _, parts, rows, features = ckpt.shape
    length = rows * ranks
    owned = features // ranks
    chunks = owned // width
    out = pl.pallas_call(
        functools.partial(kernel, sections, ranks),
        out_shape=pltpu.VMEM((parts, rows, features), jnp.bfloat16),
        in_specs=[pl.BlockSpec(memory_space=pl.ANY)] * 2,
        out_specs=pl.BlockSpec(memory_space=pltpu.VMEM),
        scratch_shapes=[
            pltpu.VMEM((chunks, parts, length, width), jnp.bfloat16),
            pltpu.VMEM((chunks, length, width), jnp.bfloat16),
            pltpu.VMEM((chunks, parts, length, width), jnp.bfloat16),
            pltpu.SemaphoreType.DMA,
            pltpu.SemaphoreType.DMA((chunks,)),
            pltpu.SemaphoreType.DMA,
            pltpu.SemaphoreType.DMA((chunks,)),
            pltpu.SemaphoreType.DMA,
            pltpu.SemaphoreType.DMA,
            pltpu.SemaphoreType.REGULAR,
        ],
        compiler_params=pltpu.CompilerParams(
            collective_id=0, has_side_effects=True, vmem_limit_bytes=59 * 2**20
        ),
    )(ckpt[0], grad[0])
    return out[None]


def solution(mesh):
    in_specs = (P("pipe", None, "tp", None), P("pipe", "tp", None))
    out_specs = P("pipe", None, "tp", None)
    return jax.shard_map(
        on_device, mesh=mesh, in_specs=in_specs, out_specs=out_specs, check_vma=False
    )
```

```python
import functools

import jax
import jax.numpy as jnp
from jax import lax
from jax.experimental import pallas as pl
from jax.experimental.pallas import tpu as pltpu
from jax.sharding import PartitionSpec as P

HEAD_DIM = 128
MESH = pl.DeviceIdType.MESH
GREETER = 4
ANSWERER = 2
PACE = 3
NT = (((1,), (1,)), ((), ()))
NN = (((1,), (0,)), ((), ()))
TN = (((0,), (0,)), ((), ()))


def dot(a, b, dims):
    return lax.dot_general(a, b, dims, preferred_element_type=jnp.float32)


def head_back(q, k, v, g):
    length = q.shape[0]
    scale = HEAD_DIM ** (-0.5)
    scores = dot(q, k, NT) * scale
    rows = lax.broadcasted_iota(jnp.int32, (length, length), 0)
    cols = lax.broadcasted_iota(jnp.int32, (length, length), 1)
    scores = jnp.where(cols <= rows, scores, jnp.float32(-1e30))
    top = jnp.max(scores, axis=-1, keepdims=True)
    expd = jnp.exp(scores - top)
    probs = expd / jnp.sum(expd, axis=-1, keepdims=True)
    probs_b = probs.astype(jnp.bfloat16)
    dprobs = dot(g, v, NT)
    delta = jnp.sum(probs_b.astype(jnp.float32) * dprobs, axis=-1, keepdims=True)
    dscores = (probs * (dprobs - delta) * scale).astype(jnp.bfloat16)
    dq = dot(dscores, k, NN)
    dk = dot(dscores, q, TN)
    dv = dot(probs_b, g, TN)
    return dq, dk, dv


def kernel(sections, ranks, ckpt, grad, out, qkv, gbuf, obuf, msend, mrecv, gsend, grecv, osend, orecv, ready):
    p = lax.axis_index("pipe")
    t = lax.axis_index("tp")
    mirror = sections - 1 - p
    rows = ckpt.shape[1]
    owned = ckpt.shape[2] // ranks
    chunks = qkv.shape[0]
    width = qkv.shape[3]
    mine = pl.ds(pl.multiple_of(t * rows, rows), rows)

    def peer(k):
        return lax.rem(t + k, ranks)

    def features(rank, c):
        return pl.ds(pl.multiple_of(rank * owned + c * width, width), width)

    def fetch_grad(c):
        pltpu.make_async_copy(grad.at[:, features(t, c)], gbuf.at[c, mine, :], grecv.at[c]).start()
        for k in range(1, ranks):
            pltpu.make_async_remote_copy(
                src_ref=grad.at[:, features(peer(k), c)],
                dst_ref=gbuf.at[c, mine, :],
                send_sem=gsend,
                recv_sem=grecv.at[c],
                device_id=(p, peer(k)),
                device_id_type=MESH,
            ).start()

    def fetch_mirror(c):
        for k in range(ranks):
            pltpu.make_async_remote_copy(
                src_ref=ckpt.at[:, :, features(peer(k), c)],
                dst_ref=qkv.at[c, :, mine, :],
                send_sem=msend,
                recv_sem=mrecv.at[c],
                device_id=(mirror, peer(k)),
                device_id_type=MESH,
            ).start()

    place = lax.div(p, 16) + lax.rem(lax.div(p, 4), 4)
    half = lax.rem(lax.div(p, 2), 2)
    answers = 2 * place + 9 * half >= 11
    barrier = pltpu.get_barrier_semaphore()
    for k in range(1, ranks):
        pl.semaphore_signal(barrier, inc=1, device_id=(p, peer(k)), device_id_type=MESH)

    @pl.when(jnp.logical_not(answers))
    def _():
        for k in range(ranks):
            pl.semaphore_signal(barrier, inc=1, device_id=(mirror, peer(k)), device_id_type=MESH)
        pl.semaphore_wait(barrier, ranks - 1)

    @pl.when(answers)
    def _():
        pl.semaphore_wait(barrier, 2 * ranks - 1)
        for k in range(ranks):
            pl.semaphore_signal(ready, inc=1, device_id=(mirror, peer(k)), device_id_type=MESH)

    early = lax.select(answers, ANSWERER, GREETER)

    @pl.loop(0, early)
    def _(c):
        fetch_grad(c)

    @pl.when(jnp.logical_not(answers))
    def _():
        pl.semaphore_wait(ready, ranks)

    @pl.loop(0, chunks)
    def _(c):
        fetch_mirror(c)

        for j in range(PACE):
            @pl.when(early + c * PACE + j < chunks)
            def _():
                fetch_grad(early + c * PACE + j)

    def arrived(ref, sem):
        pltpu.make_async_copy(ref, ref, sem).wait()

    @pl.loop(0, chunks)
    def _(c):
        arrived(qkv.at[c], mrecv.at[c])
        arrived(gbuf.at[c], grecv.at[c])

        for h in range(width // HEAD_DIM):
            lanes = slice(h * HEAD_DIM, (h + 1) * HEAD_DIM)
            dq, dk, dv = head_back(qkv[c, 0, :, lanes], qkv[c, 1, :, lanes], qkv[c, 2, :, lanes], gbuf[c, :, lanes])
            obuf[c, 0, :, lanes] = dq.astype(jnp.bfloat16)
            obuf[c, 1, :, lanes] = dk.astype(jnp.bfloat16)
            obuf[c, 2, :, lanes] = dv.astype(jnp.bfloat16)

        for k in range(1, ranks):
            theirs = pl.ds(pl.multiple_of(peer(k) * rows, rows), rows)
            pltpu.make_async_remote_copy(
                src_ref=obuf.at[c, :, theirs, :],
                dst_ref=out.at[:, :, features(t, c)],
                send_sem=osend,
                recv_sem=orecv,
                device_id=(p, peer(k)),
                device_id_type=MESH,
            ).start()
        pltpu.make_async_copy(obuf.at[c, :, mine, :], out.at[:, :, features(t, c)], orecv).start()

    arrived(ckpt, msend)
    most = pl.ds(0, (ranks - 1) * owned)
    arrived(grad.at[:, most], gsend)
    arrived(out.at[:, :, most], osend)
    arrived(out, orecv)


def on_device(ckpt, grad, width=HEAD_DIM):
    sections = lax.axis_size("pipe")
    ranks = lax.axis_size("tp")
    _, parts, rows, features = ckpt.shape
    length = rows * ranks
    owned = features // ranks
    chunks = owned // width
    out = pl.pallas_call(
        functools.partial(kernel, sections, ranks),
        out_shape=pltpu.VMEM((parts, rows, features), jnp.bfloat16),
        in_specs=[pl.BlockSpec(memory_space=pl.ANY)] * 2,
        out_specs=pl.BlockSpec(memory_space=pltpu.VMEM),
        scratch_shapes=[
            pltpu.VMEM((chunks, parts, length, width), jnp.bfloat16),
            pltpu.VMEM((chunks, length, width), jnp.bfloat16),
            pltpu.VMEM((chunks, parts, length, width), jnp.bfloat16),
            pltpu.SemaphoreType.DMA,
            pltpu.SemaphoreType.DMA((chunks,)),
            pltpu.SemaphoreType.DMA,
            pltpu.SemaphoreType.DMA((chunks,)),
            pltpu.SemaphoreType.DMA,
            pltpu.SemaphoreType.DMA,
            pltpu.SemaphoreType.REGULAR,
        ],
        compiler_params=pltpu.CompilerParams(
            collective_id=0, has_side_effects=True, vmem_limit_bytes=59 * 2**20
        ),
    )(ckpt[0], grad[0])
    return out[None]


def solution(mesh):
    in_specs = (P("pipe", None, "tp", None), P("pipe", "tp", None))
    out_specs = P("pipe", None, "tp", None)
    return jax.shard_map(
        on_device, mesh=mesh, in_specs=in_specs, out_specs=out_specs, check_vma=False
    )
```
